256 devices in a mesh: grp: 8 (over y, x_lo), ep: 32 (over x_hi, z, core).
Axes of the slice: x: 4 (x_hi: 2, x_lo: 2; x = x_hi * 2 + x_lo), y: 4, z: 8, core: 2. Of those that a mesh axis runs over, the one named last changes fastest.
Arguments:
- queries: bfloat16 [8, 32, 384, 5120], P('grp', 'ep'), may hold values from -8 to 8
- suffix_kv: bfloat16 [8, 32, 2, 384, 1024], P('grp', 'ep'), may hold values from -6 to 6
- slot_page_cache: bfloat16 [8, 32, 16, 2, 16, 1024], P('grp', 'ep'), may hold values from -6 to 6
- holder: int32 [8, 32], replicated, may hold values from 0 to 7, as said below
- page_slots: int32 [8, 32, 32], replicated, may hold values from 0 to 15
- page_count: int32 [8, 32], replicated, may hold values from 1 to 32
Outputs:
- attended: bfloat16 [8, 32, 384, 5120], P('grp', 'ep')
The draws below stay inside these ranges and needn't reach their ends.
Inputs may be any that keep to these rules, and one draw needn't show every extreme that they name: In every group exactly 8 requests share one holder group and no holder group serves more than 8 requests of one group.
All inputs are finite; a program needn't handle non-finite values.
Results may differ from the reference program's by a relative error of at most 0.005.
Values may be sent and summed in bfloat16 or wider, within the bound.
No kernel may reach another device: no remote copies, remote signals or barrier semaphores. Data moves between devices by JAX's collectives and lax.ppermute only.
A program may use at most 128 MiB of HBM per device.

```python
import jax
import jax.numpy as jnp
from jax import lax

QUERY_HEAD_COUNT = 40
KEY_VALUE_HEADS = 8
HEAD_SIZE = 128
SUFFIX_TOKENS = 384
PAGE_TOKENS = 16
DEVICE_SLOTS = 16
SERVING_GROUPS = 8
GROUP_REQUESTS = 32
N_GRP = 8
N_EP = 32


def draw_suffix_kv(key, part):
    key = jax.random.fold_in(key, 11)
    complete_shape = (SERVING_GROUPS, GROUP_REQUESTS, 2, SUFFIX_TOKENS, KEY_VALUE_HEADS * HEAD_SIZE)
    drawn = jnp.clip(jax.random.normal(key, complete_shape, jnp.float32), -6.0, 6.0)
    return drawn.astype(jnp.bfloat16)


def draw_queries(key, part):
    key = jax.random.fold_in(key, 12)
    complete_shape = (SERVING_GROUPS, GROUP_REQUESTS, SUFFIX_TOKENS, QUERY_HEAD_COUNT * HEAD_SIZE)
    drawn = jnp.clip(2.0 * jax.random.normal(key, complete_shape, jnp.float32), -8.0, 8.0)
    return drawn.astype(jnp.bfloat16)


def draw_holder(key, part):
    key = jax.random.fold_in(key, 13)
    slot_cap = GROUP_REQUESTS // 4

    def one_group(group_key):
        first, second, third = jax.random.split(group_key, 3)
        heavy = jax.random.randint(first, (), 0, SERVING_GROUPS).astype(jnp.int32)
        others = (jax.random.permutation(second, (SERVING_GROUPS - 1) * slot_cap)[:GROUP_REQUESTS - slot_cap] // slot_cap).astype(jnp.int32)
        others = others + (others >= heavy).astype(jnp.int32)
        listed = jnp.concatenate([jnp.full((slot_cap,), heavy, jnp.int32), others])
        return jax.random.permutation(third, listed)
    return jax.vmap(one_group)(jax.random.split(key, SERVING_GROUPS)).astype(jnp.int32)


def place_ends(result, own_key, low, high):
    shape = result.shape
    place = [jax.random.randint(jax.random.fold_in(own_key, axis), (), 0, shape[axis]) for axis in range(len(shape))]
    result = result.at[tuple(place)].set(low)
    longest = shape.index(max(shape))
    place[longest] = (place[longest] + 1) % shape[longest]
    return result.at[tuple(place)].set(high)


def shard_levels(rng, extent, cuts, low, top_value):
    def one(axis_at, blocks):
        draws = jax.random.uniform(jax.random.fold_in(jax.random.fold_in(rng, 6), axis_at), (blocks,), jnp.float32, low / len(cuts), top_value / len(cuts))
        return jnp.repeat(jnp.exp(draws), extent[axis_at] // blocks).reshape((-1,) + (1,) * (len(extent) - axis_at - 1))

    level = one(*cuts[0])
    for cut in cuts[1:]:
        level = level * one(*cut)
    return level


def scatter_about(stream_key, shape, width, reach, shards=(), held_as=jnp.bfloat16):
    result = jax.random.normal(stream_key, shape, jnp.float32) * width
    if len(shards) > 0:
        result = shard_levels(stream_key, shape, shards, -0.22, 0.18) * result
    return jnp.clip(result, min=-reach, max=reach).astype(held_as)


def setup_inputs(seed: int = 0) -> dict:
    seeds = jax.random.split(jax.random.key(seed), 7)
    return {
        "queries": draw_queries(jax.random.fold_in(seeds[6], 71), 0),
        "suffix_kv": draw_suffix_kv(jax.random.fold_in(seeds[6], 71), 0),
        "slot_page_cache": scatter_about(seeds[2], (SERVING_GROUPS, GROUP_REQUESTS, DEVICE_SLOTS, 2, PAGE_TOKENS, KEY_VALUE_HEADS * HEAD_SIZE), 1.0, 6.0, ((0, 8), (1, 32))),
        "holder": draw_holder(jax.random.fold_in(seeds[6], 71), 0),
        "page_slots": place_ends(jax.random.randint(seeds[4], (SERVING_GROUPS, GROUP_REQUESTS, GROUP_REQUESTS), 0, DEVICE_SLOTS), jax.random.fold_in(seeds[4], 1), 0, DEVICE_SLOTS - 1).astype(jnp.int32),
        "page_count": place_ends(jax.random.randint(seeds[5], (SERVING_GROUPS, GROUP_REQUESTS), 1, GROUP_REQUESTS + 1), jax.random.fold_in(seeds[5], 1), 1, GROUP_REQUESTS).astype(jnp.int32),
    }


def attend(rows_of_queries, pulled, suffix_pair, page_total):
    suffix_length = rows_of_queries.shape[0]
    page_number, pair_dim, page_len, kv_width = pulled.shape
    prefix_len = page_number * page_len
    prefix_kv = jnp.transpose(pulled, (1, 0, 2, 3)).reshape(2, prefix_len, kv_width)
    key_value_pair = jnp.concatenate([prefix_kv, suffix_pair], axis=1)
    total_keys = prefix_len + suffix_length
    group_width = QUERY_HEAD_COUNT // KEY_VALUE_HEADS
    heads_of_queries = rows_of_queries.reshape(suffix_length, KEY_VALUE_HEADS, group_width, HEAD_SIZE).transpose(1, 2, 0, 3)
    heads_of_keys = key_value_pair[0].reshape(total_keys, KEY_VALUE_HEADS, HEAD_SIZE).transpose(1, 0, 2)
    heads_of_values = key_value_pair[1].reshape(total_keys, KEY_VALUE_HEADS, HEAD_SIZE).transpose(1, 0, 2)
    key_pos = jnp.arange(total_keys)
    query_pos = jnp.arange(suffix_length)
    in_prefix = (key_pos[None, :] // page_len) < page_total
    in_suffix = (key_pos[None, :] - prefix_len) <= query_pos[:, None]
    allowed = jnp.where(key_pos[None, :] < prefix_len, in_prefix, in_suffix)
    scale = 1.0 / (HEAD_SIZE ** 0.5)

    def one_head(operands):
        q_head, k_head, v_head = operands
        scores = jnp.einsum("gsd,td->gst", q_head.astype(jnp.float32), k_head.astype(jnp.float32)) * scale
        scores = jnp.where(allowed[None], scores, -1e30)
        top_score = jnp.max(scores, axis=-1, keepdims=True)
        raised = jnp.where(allowed[None], jnp.exp(scores - top_score), 0.0)
        total = jnp.sum(raised, axis=-1, keepdims=True)
        weights = (raised / total).astype(jnp.bfloat16)
        return jnp.einsum("gst,td->gsd", weights.astype(jnp.float32), v_head.astype(jnp.float32))

    mixed = lax.map(one_head, (heads_of_queries, heads_of_keys, heads_of_values))
    mixed = mixed.transpose(2, 0, 1, 3).reshape(suffix_length, QUERY_HEAD_COUNT * HEAD_SIZE)
    return mixed.astype(jnp.bfloat16)


def reference(queries, suffix_kv, slot_page_cache, holder, page_slots, page_count):
    def per_request(request):
        group_idx = request // N_EP
        lane_idx = request % N_EP
        source = holder[group_idx, lane_idx]
        pulled = slot_page_cache[source, jnp.arange(N_EP), page_slots[group_idx, lane_idx]]
        return attend(queries[group_idx, lane_idx], pulled, suffix_kv[group_idx, lane_idx], page_count[group_idx, lane_idx])

    outputs = lax.map(per_request, jnp.arange(N_GRP * N_EP))
    return outputs.reshape(N_GRP, N_EP, SUFFIX_TOKENS, QUERY_HEAD_COUNT * HEAD_SIZE)
```

```python
import functools
import math

import jax
import jax.numpy as jnp
from jax import lax
from jax.experimental import pallas as pl
from jax.experimental.pallas import tpu as pltpu
from jax.sharding import PartitionSpec as P

HEAD = 128
KV_HEADS = 8
GROUP_HEADS = 5
PAGE = 16
CAP = 8
TILE = 128
SMEM = pltpu.MemorySpace.SMEM
NEG = -1e30


def pack_kernel(n_grp, n_ep, holder_ref, slots_ref, cache_ref, out_ref, count_ref, sem):
    me = lax.axis_index("grp")
    lane = lax.axis_index("ep")

    def group(g, carry):
        count_ref[g] = 0

        def request(e, carry):
            @pl.when(holder_ref[g, e] == me)
            def _():
                k = count_ref[g]
                at = g * CAP + k
                pltpu.make_async_copy(cache_ref.at[slots_ref[g, e]], out_ref.at[at], sem.at[at]).start()
                count_ref[g] = k + 1

            return carry

        return lax.fori_loop(0, n_ep, request, carry, unroll=8)

    lax.fori_loop(0, n_grp, group, 0)

    def drain(at, carry):
        @pl.when(lax.rem(at, CAP) < count_ref[at // CAP])
        def _():
            pltpu.make_async_copy(cache_ref.at[0], out_ref.at[at], sem.at[at]).wait()

        return carry

    lax.fori_loop(0, n_grp * CAP, drain, 0)


def pack(holder, slots, cache):
    n_grp, n_ep = holder.shape
    return pl.pallas_call(
        functools.partial(pack_kernel, n_grp, n_ep),
        out_shape=jax.ShapeDtypeStruct((n_grp * CAP,) + cache.shape[1:], cache.dtype),
        in_specs=[
            pl.BlockSpec(memory_space=SMEM),
            pl.BlockSpec(memory_space=SMEM),
            pl.BlockSpec(memory_space=pl.ANY),
        ],
        out_specs=pl.BlockSpec(memory_space=pl.ANY),
        scratch_shapes=[pltpu.SMEM((n_grp,), jnp.int32), pltpu.SemaphoreType.DMA((n_grp * CAP,))],
        name="pack_pages",
    )(holder, slots, cache)


def select_kernel(n_grp, n_ep, holder_ref, arrived_ref, out_ref, count_ref, sem):
    me = lax.axis_index("grp")

    def clear(h, carry):
        count_ref[h] = 0
        return carry

    lax.fori_loop(0, n_grp, clear, 0, unroll=True)

    def request(e, carry):
        h = holder_ref[me, e]
        k = count_ref[h]
        pltpu.make_async_copy(arrived_ref.at[h * CAP + k], out_ref.at[e], sem.at[e]).start()
        count_ref[h] = k + 1
        return carry

    lax.fori_loop(0, n_ep, request, 0, unroll=4)

    def drain(e, carry):
        pltpu.make_async_copy(arrived_ref.at[0], out_ref.at[e], sem.at[e]).wait()
        return carry

    lax.fori_loop(0, n_ep, drain, 0)


def select(holder, arrived):
    n_grp, n_ep = holder.shape
    return pl.pallas_call(
        functools.partial(select_kernel, n_grp, n_ep),
        out_shape=jax.ShapeDtypeStruct((n_ep,) + arrived.shape[1:], arrived.dtype),
        in_specs=[pl.BlockSpec(memory_space=SMEM), pl.BlockSpec(memory_space=pl.ANY)],
        out_specs=pl.BlockSpec(memory_space=pl.ANY),
        scratch_shapes=[pltpu.SMEM((n_grp,), jnp.int32), pltpu.SemaphoreType.DMA((n_ep,))],
        name="select_pages",
    )(holder, arrived)


def attend_kernel(pages, q_ref, pulled_ref, suffix_ref, count_ref, o_ref):
    prefix = pages * PAGE
    tokens = q_ref.shape[0]
    valid = count_ref[lax.axis_index("grp"), lax.axis_index("ep")] * PAGE
    ok = lax.broadcasted_iota(jnp.int32, (prefix, HEAD), 0) < valid
    k_pre = pulled_ref[:, 0].reshape(prefix, HEAD).astype(jnp.float32)
    k_pre = jnp.where(ok, k_pre, k_pre[0:1, :]).astype(jnp.bfloat16)
    v_pre = pulled_ref[:, 1].reshape(prefix, HEAD).astype(jnp.float32)
    v_pre = jnp.where(ok, v_pre, 0.0).astype(jnp.bfloat16)
    one_pre = jnp.where(ok, 1.0, 0.0).astype(jnp.bfloat16)
    keys = jnp.concatenate([k_pre, suffix_ref[0]], axis=0)
    values = jnp.concatenate(
        [
            jnp.concatenate([v_pre, one_pre], axis=1),
            jnp.concatenate([suffix_ref[1], jnp.ones((tokens, HEAD), jnp.bfloat16)], axis=1),
        ],
        axis=0,
    )
    scale = math.log2(math.e) / math.sqrt(HEAD)
    rows = GROUP_HEADS * TILE
    tri = lax.rem(lax.broadcasted_iota(jnp.int32, (rows, TILE), 0), TILE) >= lax.broadcasted_iota(
        jnp.int32, (rows, TILE), 1
    )

    for i in range(tokens // TILE):
        span = slice(i * TILE, (i + 1) * TILE)
        total = prefix + (i + 1) * TILE
        q = jnp.concatenate([q_ref[span, n * HEAD : (n + 1) * HEAD] for n in range(GROUP_HEADS)], axis=0)
        s = lax.dot_general(q, keys[:total], (((1,), (1,)), ((), ())), preferred_element_type=jnp.float32)
        s = jnp.concatenate([s[:, : total - TILE], jnp.where(tri, s[:, total - TILE :], NEG)], axis=1)
        top = jnp.max(s, axis=1, keepdims=True)
        p = jnp.exp2((s - top) * scale).astype(jnp.bfloat16)
        acc = jnp.dot(p, values[:total], preferred_element_type=jnp.float32)
        out = (acc[:, :HEAD] / acc[:, HEAD:]).astype(jnp.bfloat16)
        for n in range(GROUP_HEADS):
            o_ref[span, n * HEAD : (n + 1) * HEAD] = out[n * TILE : (n + 1) * TILE]


def attend(queries, pulled, suffix_pair, page_count):
    tokens, width = queries.shape
    pages = pulled.shape[0]
    block = GROUP_HEADS * HEAD
    return pl.pallas_call(
        functools.partial(attend_kernel, pages),
        out_shape=jax.ShapeDtypeStruct((tokens, width), jnp.bfloat16),
        grid=(KV_HEADS,),
        in_specs=[
            pl.BlockSpec((tokens, block), lambda h: (0, h)),
            pl.BlockSpec((pages, 2, PAGE, HEAD), lambda h: (0, 0, 0, h)),
            pl.BlockSpec((2, tokens, HEAD), lambda h: (0, 0, h)),
            pl.BlockSpec(memory_space=SMEM),
        ],
        out_specs=pl.BlockSpec((tokens, block), lambda h: (0, h)),
        compiler_params=pltpu.CompilerParams(vmem_limit_bytes=48 * 1024 * 1024),
        name="attend",
    )(queries, pulled, suffix_pair, page_count)


def local(queries, suffix_kv, slot_page_cache, holder, page_slots, page_count):
    lane = lax.axis_index("ep")
    slots = lax.dynamic_index_in_dim(page_slots, lane, axis=2, keepdims=False)
    outgoing = pack(holder, slots, slot_page_cache[0, 0])
    arrived = lax.all_to_all(outgoing, "grp", split_axis=0, concat_axis=0, tiled=True)
    forward = select(holder, arrived)
    pulled = lax.all_to_all(forward, "ep", split_axis=0, concat_axis=0, tiled=True)
    return attend(queries[0, 0], pulled, suffix_kv[0, 0], page_count)[None, None]


def solution(mesh):
    return jax.shard_map(
        local,
        mesh=mesh,
        in_specs=(
            P("grp", "ep", None, None),
            P("grp", "ep", None, None, None),
            P("grp", "ep", None, None, None, None),
            P(),
            P(),
            P(),
        ),
        out_specs=P("grp", "ep", None, None),
        check_vma=False,
    )
```

```python
import functools
import math

import jax
import jax.numpy as jnp
from jax import lax
from jax.experimental import pallas as pl
from jax.experimental.pallas import tpu as pltpu
from jax.sharding import PartitionSpec as P

HEAD = 128
KV_HEADS = 8
GROUP_HEADS = 5
PAGE = 16
CAP = 8
TILE = 128
SMEM = pltpu.MemorySpace.SMEM
NEG = -1e30
SCALE = math.log2(math.e) / math.sqrt(HEAD)
RING = 4
SHIFTS = [(dy, dx) for dy in range(RING) for dx in range(2)]
CHUNKS = ((0, 5), (5, 3))
ORDER = (1, 2, 3, 4, 5, 6, 7)
TIE = 2
DEPTH = 3
MIB = 1024 * 1024


def target(group, dy, dx):
    return lax.rem(group // 2 + dy, RING) * 2 + lax.rem(group + dx, 2)


def pack_kernel(n_ep, holder_ref, slots_ref, cache_ref, *rest):
    n = len(SHIFTS)
    outs = [rest[c * n : (c + 1) * n] for c in range(len(CHUNKS))]
    list_ref, held, sem, out_sem = rest[len(CHUNKS) * n :]
    me = lax.axis_index("grp")
    load = pltpu.make_async_copy(cache_ref, held, sem)
    load.start()

    def copy(c, s, slot, k):
        first, heads = CHUNKS[c]
        part = held.at[slot, :, :, pl.ds(first * HEAD, heads * HEAD)]
        return pltpu.make_async_copy(part, outs[c][s].at[k], out_sem.at[c, s, k])

    counts = []
    for s, (dy, dx) in enumerate(SHIFTS):
        g = target(me, dy, dx)

        count = jnp.int32(0)
        for base in range(0, n_ep, 8):
            span = range(base, min(base + 8, n_ep))
            mine = [(holder_ref[g, e] == me).astype(jnp.int32) for e in span]
            slot = [slots_ref[g, e] for e in span]
            for one, held_in in zip(mine, slot):
                list_ref[s, count] = held_in
                count = count + one
        counts.append(count)
        if s == 0:
            load.wait()

        def send(k, carry, s=s):
            for c in range(len(CHUNKS)):
                copy(c, s, list_ref[s, k], k).start()
            return carry

        lax.fori_loop(0, counts[s], send, 0)
    for s, count in enumerate(counts):

        def drain(k, carry, s=s):
            for c in range(len(CHUNKS)):
                copy(c, s, 0, k).wait()
            return carry

        lax.fori_loop(0, count, drain, 0)


def pack(holder, slots, cache):
    n_slots, pair, page, _ = cache.shape
    n = len(SHIFTS)
    outs = pl.pallas_call(
        functools.partial(pack_kernel, holder.shape[1]),
        out_shape=[
            jax.ShapeDtypeStruct((CAP, pair, page, heads * HEAD), cache.dtype) for _, heads in CHUNKS for _ in SHIFTS
        ],
        in_specs=[
            pl.BlockSpec(memory_space=SMEM),
            pl.BlockSpec(memory_space=SMEM),
            pl.BlockSpec(memory_space=pl.ANY),
        ],
        out_specs=[pl.BlockSpec(memory_space=pl.ANY)] * (n * len(CHUNKS)),
        scratch_shapes=[
            pltpu.SMEM((n, 2 * CAP), jnp.int32),
            pltpu.VMEM(cache.shape, cache.dtype),
            pltpu.SemaphoreType.DMA,
            pltpu.SemaphoreType.DMA((len(CHUNKS), n, CAP)),
        ],
        compiler_params=pltpu.CompilerParams(vmem_limit_bytes=63 * MIB),
        cost_estimate=pl.CostEstimate(flops=0, bytes_accessed=6 * MIB, transcendentals=0),
        name="pack_pages",
    )(holder, slots, cache)
    return [outs[c * n : (c + 1) * n] for c in range(len(CHUNKS))]


def select_kernel(n_ep, holder_ref, *rest):
    arrived, (out_ref, count_ref, held, sem, out_sem) = rest[: len(SHIFTS)], rest[len(SHIFTS) :]
    me = lax.axis_index("grp")
    loads = [pltpu.make_async_copy(arrived[s], held.at[s], sem.at[s]) for s in range(len(SHIFTS))]
    for load in loads:
        load.start()
    for s in range(len(SHIFTS)):
        count_ref[s] = 0
    for load in loads:
        load.wait()

    def request(e, carry):
        h = holder_ref[me, e]
        s = lax.rem(me // 2 - h // 2 + RING, RING) * 2 + lax.rem(me + h, 2)
        k = count_ref[s]
        pltpu.make_async_copy(held.at[s, k], out_ref.at[e], out_sem.at[e]).start()
        count_ref[s] = k + 1
        return carry

    lax.fori_loop(0, n_ep, request, 0, unroll=8)

    def drain(e, carry):
        pltpu.make_async_copy(held.at[0, 0], out_ref.at[e], out_sem.at[e]).wait()
        return carry

    lax.fori_loop(0, n_ep, drain, 0, unroll=8)


def select(holder, arrived):
    n_ep = holder.shape[1]
    one = arrived[0].shape[1:]
    dtype = arrived[0].dtype
    return pl.pallas_call(
        functools.partial(select_kernel, n_ep),
        out_shape=jax.ShapeDtypeStruct((n_ep,) + one, dtype),
        in_specs=[pl.BlockSpec(memory_space=SMEM)] + [pl.BlockSpec(memory_space=pl.ANY)] * len(SHIFTS),
        out_specs=pl.BlockSpec(memory_space=pl.ANY),
        scratch_shapes=[
            pltpu.SMEM((len(SHIFTS),), jnp.int32),
            pltpu.VMEM((len(SHIFTS), CAP) + one, dtype),
            pltpu.SemaphoreType.DMA((len(SHIFTS),)),
            pltpu.SemaphoreType.DMA((n_ep,)),
        ],
        compiler_params=pltpu.CompilerParams(vmem_limit_bytes=63 * MIB),
        cost_estimate=pl.CostEstimate(flops=0, bytes_accessed=6 * MIB, transcendentals=0),
        name="select_pages",
    )(holder, *arrived)


def triangle():
    return lax.broadcasted_iota(jnp.int32, (TILE, TILE), 0) >= lax.broadcasted_iota(jnp.int32, (TILE, TILE), 1)


def prefix_pair(pulled_ref, valid):
    prefix = pulled_ref.shape[0] * PAGE
    ok = lax.broadcasted_iota(jnp.int32, (prefix, HEAD), 0) < valid
    keys = pulled_ref[:, 0].reshape(prefix, HEAD).astype(jnp.float32)
    keys = jnp.where(ok, keys, keys[0:1, :]).astype(jnp.bfloat16)
    values = pulled_ref[:, 1].reshape(prefix, HEAD).astype(jnp.float32)
    values = jnp.where(ok, values, 0.0).astype(jnp.bfloat16)
    ones = jnp.where(ok, 1.0, 0.0).astype(jnp.bfloat16)
    return keys, jnp.concatenate([values, ones], axis=1)


def suffix_pair_of(suffix_ref):
    return suffix_ref[0], jnp.concatenate([suffix_ref[1], jnp.ones(suffix_ref.shape[1:], jnp.bfloat16)], axis=1)


def attend_kernel(q_ref, pulled_ref, suffix_ref, count_ref, *rest):
    o_ref = rest[-1]
    valid = count_ref[lax.axis_index("grp"), lax.axis_index("ep")] * PAGE
    k_pre, v_pre = prefix_pair(pulled_ref, valid)
    k_suf, v_suf = suffix_pair_of(suffix_ref)
    keys = jnp.concatenate([k_pre, k_suf], axis=0)
    values = jnp.concatenate([v_pre, v_suf], axis=0)
    tri = triangle()
    tiles = [(i, n) for i in range(q_ref.shape[0] // TILE) for n in range(GROUP_HEADS)]

    def place(tile):
        i, n = tile
        return slice(i * TILE, (i + 1) * TILE), slice(n * HEAD, (n + 1) * HEAD)

    def total(tile):
        return k_pre.shape[0] + (tile[0] + 1) * TILE

    def score(tile):
        q = q_ref[place(tile)]
        return lax.dot_general(q, keys[: total(tile)], (((1,), (1,)), ((), ())), preferred_element_type=jnp.float32)

    def weigh(tile, s):
        end = total(tile)
        s = jnp.concatenate([s[:, : end - TILE], jnp.where(tri, s[:, end - TILE :], NEG)], axis=1)
        top = jnp.max(s, axis=1, keepdims=True)
        return jnp.exp2((s - top) * SCALE).astype(jnp.bfloat16)

    def mix(tile, p):
        return jnp.dot(p, values[: total(tile)], preferred_element_type=jnp.float32)

    scores, weights, mixed = {}, {}, {}
    for t in range(len(tiles) + 3 * DEPTH):
        if t < len(tiles):
            scores[t] = score(tiles[t])
        u = t - DEPTH
        if 0 <= u < len(tiles):
            weights[u] = weigh(tiles[u], scores.pop(u))
        u -= DEPTH
        if 0 <= u < len(tiles):
            mixed[u] = mix(tiles[u], weights.pop(u))
        u -= DEPTH
        if 0 <= u < len(tiles):
            acc = mixed.pop(u)
            o_ref[place(tiles[u])] = (acc[:, :HEAD] / acc[:, HEAD:]).astype(jnp.bfloat16)


def cost(heads, keys):
    work = heads * GROUP_HEADS * 384 * keys
    return pl.CostEstimate(flops=4 * HEAD * work, bytes_accessed=heads * MIB * 3 // 2, transcendentals=work)


def attend(chunk, queries, pulled, suffix, page_count, so_far):
    first, heads = chunk
    tokens, width = queries.shape
    pages = pulled.shape[0]
    block = GROUP_HEADS * HEAD
    operands = [queries, pulled, suffix, page_count]
    in_specs = [
        pl.BlockSpec((tokens, block), lambda h: (0, first + h)),
        pl.BlockSpec((pages, 2, PAGE, HEAD), lambda h: (0, 0, 0, h)),
        pl.BlockSpec((2, tokens, HEAD), lambda h: (0, 0, first + h)),
        pl.BlockSpec(memory_space=SMEM),
    ]
    aliases = {}
    if so_far is not None:
        aliases = {len(operands): 0}
        operands.append(so_far)
        in_specs.append(pl.BlockSpec(memory_space=pl.ANY))
    return pl.pallas_call(
        attend_kernel,
        out_shape=jax.ShapeDtypeStruct((tokens, width), jnp.bfloat16),
        grid=(heads,),
        in_specs=in_specs,
        out_specs=pl.BlockSpec((tokens, block), lambda h: (0, first + h)),
        input_output_aliases=aliases,
        compiler_params=pltpu.CompilerParams(vmem_limit_bytes=63 * MIB),
        cost_estimate=cost(heads, 768),
        name="attend",
    )(*operands)


def shift(page, dy, dx):
    pairs = [(y * 2 + x, (y + dy) % RING * 2 + (x + dx) % 2) for y in range(RING) for x in range(2)]
    return lax.ppermute(page, "grp", pairs)


def exchange(pages):
    return lax.all_to_all(pages, "ep", split_axis=0, concat_axis=0, tiled=True)


def local(queries, suffix_kv, slot_page_cache, holder, page_slots, page_count):
    lane = lax.axis_index("ep")
    slots = lax.dynamic_index_in_dim(page_slots, lane, axis=2, keepdims=False)
    q, suffix = queries[0, 0], suffix_kv[0, 0]
    arrived = []
    for pages in pack(holder, slots, slot_page_cache[0, 0]):
        got = {0: pages[0]}
        for s in ORDER:
            got[s] = shift(pages[s], *SHIFTS[s])
        arrived.append([got[s] for s in range(len(SHIFTS))])
    pulled = []
    for c in range(len(CHUNKS)):
        forward = select(holder, arrived[c])
        if TIE and c + 1 < len(CHUNKS):
            tied = [arrived[c + 1][s] for s in ORDER[:TIE]]
            forward, tied = lax.optimization_barrier((forward, tied))
            for s, t in zip(ORDER[:TIE], tied):
                arrived[c + 1][s] = t
        pulled.append(exchange(forward))
    out = None
    for c, chunk in enumerate(CHUNKS):
        out = attend(chunk, q, pulled[c], suffix, page_count, out)
    return out[None, None]


def solution(mesh):
    return jax.shard_map(
        local,
        mesh=mesh,
        in_specs=(
            P("grp", "ep", None, None),
            P("grp", "ep", None, None, None),
            P("grp", "ep", None, None, None, None),
            P(),
            P(),
            P(),
        ),
        out_specs=P("grp", "ep", None, None),
        check_vma=False,
    )
```

```python
import functools
import math

import jax
import jax.numpy as jnp
from jax import lax
from jax.experimental import pallas as pl
from jax.experimental.pallas import tpu as pltpu
from jax.sharding import PartitionSpec as P

HEAD = 128
KV_HEADS = 8
GROUP_HEADS = 5
PAGE = 16
CAP = 8
TILE = 128
SMEM = pltpu.MemorySpace.SMEM
NEG = -1e30
SCALE = math.log2(math.e) / math.sqrt(HEAD)
RING = 4
SHIFTS = [(dy, dx) for dy in range(RING) for dx in range(2)]
CHUNKS = ((0, 5), (5, 3))
ORDER = (1, 2, 3, 4, 5, 6, 7)
TIE = 1
DEPTH = 3
MIB = 1024 * 1024


def target(group, dy, dx):
    return lax.rem(group // 2 + dy, RING) * 2 + lax.rem(group + dx, 2)


def pack_kernel(n_ep, holder_ref, slots_ref, cache_ref, *rest):
    n = len(SHIFTS)
    outs = [rest[c * n : (c + 1) * n] for c in range(len(CHUNKS))]
    list_ref, held, sem, out_sem = rest[len(CHUNKS) * n :]
    me = lax.axis_index("grp")
    load = pltpu.make_async_copy(cache_ref, held, sem)
    load.start()

    def copy(c, s, slot, k):
        first, heads = CHUNKS[c]
        part = held.at[slot, :, :, pl.ds(first * HEAD, heads * HEAD)]
        return pltpu.make_async_copy(part, outs[c][s].at[k], out_sem.at[c, s, k])

    counts = []
    for s, (dy, dx) in enumerate(SHIFTS):
        g = target(me, dy, dx)

        count = jnp.int32(0)
        for base in range(0, n_ep, 8):
            span = range(base, min(base + 8, n_ep))
            mine = [(holder_ref[g, e] == me).astype(jnp.int32) for e in span]
            slot = [slots_ref[g, e] for e in span]
            for one, held_in in zip(mine, slot):
                list_ref[s, count] = held_in
                count = count + one
        counts.append(count)
        if s == 0:
            load.wait()

        def send(k, carry, s=s):
            for c in range(len(CHUNKS)):
                copy(c, s, list_ref[s, k], k).start()
            return carry

        lax.fori_loop(0, counts[s], send, 0)
    for s, count in enumerate(counts):

        def drain(k, carry, s=s):
            for c in range(len(CHUNKS)):
                copy(c, s, 0, k).wait()
            return carry

        lax.fori_loop(0, count, drain, 0)


def pack(holder, slots, cache):
    n_slots, pair, page, _ = cache.shape
    n = len(SHIFTS)
    outs = pl.pallas_call(
        functools.partial(pack_kernel, holder.shape[1]),
        out_shape=[
            jax.ShapeDtypeStruct((CAP, pair, page, heads * HEAD), cache.dtype) for _, heads in CHUNKS for _ in SHIFTS
        ],
        in_specs=[
            pl.BlockSpec(memory_space=SMEM),
            pl.BlockSpec(memory_space=SMEM),
            pl.BlockSpec(memory_space=pl.ANY),
        ],
        out_specs=[pl.BlockSpec(memory_space=pl.ANY)] * (n * len(CHUNKS)),
        scratch_shapes=[
            pltpu.SMEM((n, 2 * CAP), jnp.int32),
            pltpu.VMEM(cache.shape, cache.dtype),
            pltpu.SemaphoreType.DMA,
            pltpu.SemaphoreType.DMA((len(CHUNKS), n, CAP)),
        ],
        compiler_params=pltpu.CompilerParams(vmem_limit_bytes=63 * MIB),
        cost_estimate=pl.CostEstimate(flops=0, bytes_accessed=6 * MIB, transcendentals=0),
        name="pack_pages",
    )(holder, slots, cache)
    return [outs[c * n : (c + 1) * n] for c in range(len(CHUNKS))]


def select_kernel(n_ep, holder_ref, *rest):
    arrived, (out_ref, count_ref, held, sem, out_sem) = rest[: len(SHIFTS)], rest[len(SHIFTS) :]
    me = lax.axis_index("grp")
    loads = [pltpu.make_async_copy(arrived[s], held.at[s], sem.at[s]) for s in range(len(SHIFTS))]
    for load in loads:
        load.start()
    for s in range(len(SHIFTS)):
        count_ref[s] = 0
    for load in loads:
        load.wait()

    def request(e, carry):
        h = holder_ref[me, e]
        s = lax.rem(me // 2 - h // 2 + RING, RING) * 2 + lax.rem(me + h, 2)
        k = count_ref[s]
        pltpu.make_async_copy(held.at[s, k], out_ref.at[e], out_sem.at[e]).start()
        count_ref[s] = k + 1
        return carry

    lax.fori_loop(0, n_ep, request, 0, unroll=8)

    def drain(e, carry):
        pltpu.make_async_copy(held.at[0, 0], out_ref.at[e], out_sem.at[e]).wait()
        return carry

    lax.fori_loop(0, n_ep, drain, 0, unroll=8)


def select(holder, arrived):
    n_ep = holder.shape[1]
    one = arrived[0].shape[1:]
    dtype = arrived[0].dtype
    return pl.pallas_call(
        functools.partial(select_kernel, n_ep),
        out_shape=jax.ShapeDtypeStruct((n_ep,) + one, dtype),
        in_specs=[pl.BlockSpec(memory_space=SMEM)] + [pl.BlockSpec(memory_space=pl.ANY)] * len(SHIFTS),
        out_specs=pl.BlockSpec(memory_space=pl.ANY),
        scratch_shapes=[
            pltpu.SMEM((len(SHIFTS),), jnp.int32),
            pltpu.VMEM((len(SHIFTS), CAP) + one, dtype),
            pltpu.SemaphoreType.DMA((len(SHIFTS),)),
            pltpu.SemaphoreType.DMA((n_ep,)),
        ],
        compiler_params=pltpu.CompilerParams(vmem_limit_bytes=63 * MIB),
        cost_estimate=pl.CostEstimate(flops=0, bytes_accessed=6 * MIB, transcendentals=0),
        name="select_pages",
    )(holder, *arrived)


def triangle():
    return lax.broadcasted_iota(jnp.int32, (TILE, TILE), 0) >= lax.broadcasted_iota(jnp.int32, (TILE, TILE), 1)


def prefix_pair(pulled_ref, pages, valid):
    prefix = pages * PAGE
    ok = lax.broadcasted_iota(jnp.int32, (prefix, HEAD), 0) < valid
    keys = pulled_ref[:pages, 0].reshape(prefix, HEAD).astype(jnp.float32)
    keys = jnp.where(ok, keys, keys[0:1, :]).astype(jnp.bfloat16)
    values = pulled_ref[:pages, 1].reshape(prefix, HEAD).astype(jnp.float32)
    values = jnp.where(ok, values, 0.0).astype(jnp.bfloat16)
    ones = jnp.where(ok, 1.0, 0.0).astype(jnp.bfloat16)
    return keys, jnp.concatenate([values, ones], axis=1)


def suffix_pair_of(suffix_ref):
    return suffix_ref[0], jnp.concatenate([suffix_ref[1], jnp.ones(suffix_ref.shape[1:], jnp.bfloat16)], axis=1)


def attend_kernel(q_ref, pulled_ref, suffix_ref, count_ref, *rest):
    valid = count_ref[lax.axis_index("grp"), lax.axis_index("ep")] * PAGE
    for pages in range(TILE // PAGE, pulled_ref.shape[0] + 1, TILE // PAGE):
        end = pages * PAGE

        @pl.when((valid > end - TILE) & (valid <= end))
        def _(pages=pages):
            attend_pages(pages, valid, q_ref, pulled_ref, suffix_ref, rest[-1])


def attend_pages(pages, valid, q_ref, pulled_ref, suffix_ref, o_ref):
    k_pre, v_pre = prefix_pair(pulled_ref, pages, valid)
    k_suf, v_suf = suffix_pair_of(suffix_ref)
    keys = jnp.concatenate([k_pre, k_suf], axis=0)
    values = jnp.concatenate([v_pre, v_suf], axis=0)
    tri = triangle()
    tiles = [(i, n) for i in range(q_ref.shape[0] // TILE) for n in range(GROUP_HEADS)]

    def place(tile):
        i, n = tile
        return slice(i * TILE, (i + 1) * TILE), slice(n * HEAD, (n + 1) * HEAD)

    def total(tile):
        return k_pre.shape[0] + (tile[0] + 1) * TILE

    def score(tile):
        q = q_ref[place(tile)]
        return lax.dot_general(q, keys[: total(tile)], (((1,), (1,)), ((), ())), preferred_element_type=jnp.float32)

    def weigh(tile, s):
        end = total(tile)
        s = jnp.concatenate([s[:, : end - TILE], jnp.where(tri, s[:, end - TILE :], NEG)], axis=1)
        top = jnp.max(s, axis=1, keepdims=True)
        return jnp.exp2((s - top) * SCALE).astype(jnp.bfloat16)

    def mix(tile, p):
        return jnp.dot(p, values[: total(tile)], preferred_element_type=jnp.float32)

    scores, weights, mixed = {}, {}, {}
    for t in range(len(tiles) + 3 * DEPTH):
        if t < len(tiles):
            scores[t] = score(tiles[t])
        u = t - DEPTH
        if 0 <= u < len(tiles):
            weights[u] = weigh(tiles[u], scores.pop(u))
        u -= DEPTH
        if 0 <= u < len(tiles):
            mixed[u] = mix(tiles[u], weights.pop(u))
        u -= DEPTH
        if 0 <= u < len(tiles):
            acc = mixed.pop(u)
            o_ref[place(tiles[u])] = (acc[:, :HEAD] / acc[:, HEAD:]).astype(jnp.bfloat16)


def cost(heads, keys):
    work = heads * GROUP_HEADS * 384 * keys
    return pl.CostEstimate(flops=4 * HEAD * work, bytes_accessed=heads * MIB * 3 // 2, transcendentals=work)


def attend(chunk, queries, pulled, suffix, page_count, so_far):
    first, heads = chunk
    tokens, width = queries.shape
    pages = pulled.shape[0]
    block = GROUP_HEADS * HEAD
    operands = [queries, pulled, suffix, page_count]
    in_specs = [
        pl.BlockSpec((tokens, block), lambda h: (0, first + h)),
        pl.BlockSpec((pages, 2, PAGE, HEAD), lambda h: (0, 0, 0, h)),
        pl.BlockSpec((2, tokens, HEAD), lambda h: (0, 0, first + h)),
        pl.BlockSpec(memory_space=SMEM),
    ]
    aliases = {}
    if so_far is not None:
        aliases = {len(operands): 0}
        operands.append(so_far)
        in_specs.append(pl.BlockSpec(memory_space=pl.ANY))
    return pl.pallas_call(
        attend_kernel,
        out_shape=jax.ShapeDtypeStruct((tokens, width), jnp.bfloat16),
        grid=(heads,),
        in_specs=in_specs,
        out_specs=pl.BlockSpec((tokens, block), lambda h: (0, first + h)),
        input_output_aliases=aliases,
        compiler_params=pltpu.CompilerParams(vmem_limit_bytes=63 * MIB + 480 * 1024),
        cost_estimate=cost(heads, 768),
        name="attend",
    )(*operands)


def shift(page, dy, dx):
    pairs = [(y * 2 + x, (y + dy) % RING * 2 + (x + dx) % 2) for y in range(RING) for x in range(2)]
    return lax.ppermute(page, "grp", pairs)


def exchange(pages):
    return lax.all_to_all(pages, "ep", split_axis=0, concat_axis=0, tiled=True)


def local(queries, suffix_kv, slot_page_cache, holder, page_slots, page_count):
    lane = lax.axis_index("ep")
    slots = lax.dynamic_index_in_dim(page_slots, lane, axis=2, keepdims=False)
    q, suffix = queries[0, 0], suffix_kv[0, 0]
    arrived = []
    for pages in pack(holder, slots, slot_page_cache[0, 0]):
        got = {0: pages[0]}
        for s in ORDER:
            got[s] = shift(pages[s], *SHIFTS[s])
        arrived.append([got[s] for s in range(len(SHIFTS))])
    pulled = []
    for c in range(len(CHUNKS)):
        forward = select(holder, arrived[c])
        if TIE and c + 1 < len(CHUNKS):
            tied = [arrived[c + 1][s] for s in ORDER[:TIE]]
            forward, tied = lax.optimization_barrier((forward, tied))
            for s, t in zip(ORDER[:TIE], tied):
                arrived[c + 1][s] = t
        pulled.append(exchange(forward))
    out = None
    for c, chunk in enumerate(CHUNKS):
        out = attend(chunk, q, pulled[c], suffix, page_count, out)
    return out[None, None]


def solution(mesh):
    return jax.shard_map(
        local,
        mesh=mesh,
        in_specs=(
            P("grp", "ep", None, None),
            P("grp", "ep", None, None, None),
            P("grp", "ep", None, None, None, None),
            P(),
            P(),
            P(),
        ),
        out_specs=P("grp", "ep", None, None),
        check_vma=False,
    )
```

```python
import functools
import math

import jax
import jax.numpy as jnp
from jax import lax
from jax.experimental import pallas as pl
from jax.experimental.pallas import tpu as pltpu
from jax.sharding import PartitionSpec as P

HEAD = 128
KV_HEADS = 8
GROUP_HEADS = 5
PAGE = 16
CAP = 8
TILE = 128
SMEM = pltpu.MemorySpace.SMEM
NEG = -1e30
SCALE = math.log2(math.e) / math.sqrt(HEAD)
RING = 4
SHIFTS = [(dy, dx) for dy in range(RING) for dx in range(2)]
CHUNKS = ((0, 5), (5, 3))
ORDER = (1, 2, 3, 4, 5, 6, 7)
TIE = 1
ORDERS = ((0, 2, 6, 1, 5, 3, 7, 4), (0, 1, 2, 3, 4, 5, 6, 7))
DEPTH = 3
MIB = 1024 * 1024


def target(group, dy, dx):
    return lax.rem(group // 2 + dy, RING) * 2 + lax.rem(group + dx, 2)


def pack_kernel(n_ep, holder_ref, slots_ref, cache_ref, *rest):
    n = len(SHIFTS)
    outs = [rest[c * n : (c + 1) * n] for c in range(len(CHUNKS))]
    list_ref, held, sem, out_sem = rest[len(CHUNKS) * n :]
    me = lax.axis_index("grp")
    load = pltpu.make_async_copy(cache_ref, held, sem)
    load.start()

    def copy(c, s, slot, k):
        first, heads = CHUNKS[c]
        part = held.at[slot, :, :, pl.ds(first * HEAD, heads * HEAD)]
        return pltpu.make_async_copy(part, outs[c][s].at[k], out_sem.at[c, s, k])

    counts = []
    for s, (dy, dx) in enumerate(SHIFTS):
        g = target(me, dy, dx)

        count = jnp.int32(0)
        for base in range(0, n_ep, 8):
            span = range(base, min(base + 8, n_ep))
            mine = [(holder_ref[g, e] == me).astype(jnp.int32) for e in span]
            slot = [slots_ref[g, e] for e in span]
            for one, held_in in zip(mine, slot):
                list_ref[s, count] = held_in
                count = count + one
        counts.append(count)
        if s == 0:
            load.wait()

        def send(k, carry, s=s):
            for c in range(len(CHUNKS)):
                copy(c, s, list_ref[s, k], k).start()
            return carry

        lax.fori_loop(0, counts[s], send, 0)
    for s, count in enumerate(counts):

        def drain(k, carry, s=s):
            for c in range(len(CHUNKS)):
                copy(c, s, 0, k).wait()
            return carry

        lax.fori_loop(0, count, drain, 0)


def pack(holder, slots, cache):
    n_slots, pair, page, _ = cache.shape
    n = len(SHIFTS)
    outs = pl.pallas_call(
        functools.partial(pack_kernel, holder.shape[1]),
        out_shape=[
            jax.ShapeDtypeStruct((CAP, pair, page, heads * HEAD), cache.dtype) for _, heads in CHUNKS for _ in SHIFTS
        ],
        in_specs=[
            pl.BlockSpec(memory_space=SMEM),
            pl.BlockSpec(memory_space=SMEM),
            pl.BlockSpec(memory_space=pl.ANY),
        ],
        out_specs=[pl.BlockSpec(memory_space=pl.ANY)] * (n * len(CHUNKS)),
        scratch_shapes=[
            pltpu.SMEM((n, 2 * CAP), jnp.int32),
            pltpu.VMEM(cache.shape, cache.dtype),
            pltpu.SemaphoreType.DMA,
            pltpu.SemaphoreType.DMA((len(CHUNKS), n, CAP)),
        ],
        compiler_params=pltpu.CompilerParams(vmem_limit_bytes=63 * MIB),
        cost_estimate=pl.CostEstimate(flops=0, bytes_accessed=6 * MIB, transcendentals=0),
        name="pack_pages",
    )(holder, slots, cache)
    return [outs[c * n : (c + 1) * n] for c in range(len(CHUNKS))]


def select_kernel(order, n_ep, holder_ref, *rest):
    arrived, (out_ref, count_ref, held, sem, out_sem) = rest[: len(SHIFTS)], rest[len(SHIFTS) :]
    me = lax.axis_index("grp")
    loads = [pltpu.make_async_copy(pages, held.at[s], sem.at[s]) for pages, s in zip(arrived, order)]
    for load in loads:
        load.start()
    for s in range(len(SHIFTS)):
        count_ref[s] = 0
    for load in loads:
        load.wait()

    def request(e, carry):
        h = holder_ref[me, e]
        s = lax.rem(me // 2 - h // 2 + RING, RING) * 2 + lax.rem(me + h, 2)
        k = count_ref[s]
        pltpu.make_async_copy(held.at[s, k], out_ref.at[e], out_sem.at[e]).start()
        count_ref[s] = k + 1
        return carry

    lax.fori_loop(0, n_ep, request, 0, unroll=8)

    def drain(e, carry):
        pltpu.make_async_copy(held.at[0, 0], out_ref.at[e], out_sem.at[e]).wait()
        return carry

    lax.fori_loop(0, n_ep, drain, 0, unroll=8)


def select(order, holder, arrived):
    n_ep = holder.shape[1]
    one = arrived[0].shape[1:]
    dtype = arrived[0].dtype
    return pl.pallas_call(
        functools.partial(select_kernel, order, n_ep),
        out_shape=jax.ShapeDtypeStruct((n_ep,) + one, dtype),
        in_specs=[pl.BlockSpec(memory_space=SMEM)] + [pl.BlockSpec(memory_space=pl.ANY)] * len(SHIFTS),
        out_specs=pl.BlockSpec(memory_space=pl.ANY),
        scratch_shapes=[
            pltpu.SMEM((len(SHIFTS),), jnp.int32),
            pltpu.VMEM((len(SHIFTS), CAP) + one, dtype),
            pltpu.SemaphoreType.DMA((len(SHIFTS),)),
            pltpu.SemaphoreType.DMA((n_ep,)),
        ],
        compiler_params=pltpu.CompilerParams(vmem_limit_bytes=63 * MIB),
        cost_estimate=pl.CostEstimate(flops=0, bytes_accessed=6 * MIB, transcendentals=0),
        name="select_pages",
    )(holder, *[arrived[s] for s in order])


def triangle():
    return lax.broadcasted_iota(jnp.int32, (TILE, TILE), 0) >= lax.broadcasted_iota(jnp.int32, (TILE, TILE), 1)


def prefix_pair(pulled_ref, pages, valid):
    prefix = pages * PAGE
    ok = lax.broadcasted_iota(jnp.int32, (prefix, HEAD), 0) < valid
    keys = pulled_ref[:pages, 0].reshape(prefix, HEAD).astype(jnp.float32)
    keys = jnp.where(ok, keys, keys[0:1, :]).astype(jnp.bfloat16)
    values = pulled_ref[:pages, 1].reshape(prefix, HEAD).astype(jnp.float32)
    values = jnp.where(ok, values, 0.0).astype(jnp.bfloat16)
    ones = jnp.where(ok, 1.0, 0.0).astype(jnp.bfloat16)
    return keys, jnp.concatenate([values, ones], axis=1)


def suffix_pair_of(suffix_ref):
    return suffix_ref[0], jnp.concatenate([suffix_ref[1], jnp.ones(suffix_ref.shape[1:], jnp.bfloat16)], axis=1)


def attend_kernel(q_ref, pulled_ref, suffix_ref, count_ref, *rest):
    valid = count_ref[lax.axis_index("grp"), lax.axis_index("ep")] * PAGE
    for pages in range(TILE // PAGE, pulled_ref.shape[0] + 1, TILE // PAGE):
        end = pages * PAGE

        @pl.when((valid > end - TILE) & (valid <= end))
        def _(pages=pages):
            attend_pages(pages, valid, q_ref, pulled_ref, suffix_ref, rest[-1])


def attend_pages(pages, valid, q_ref, pulled_ref, suffix_ref, o_ref):
    k_pre, v_pre = prefix_pair(pulled_ref, pages, valid)
    k_suf, v_suf = suffix_pair_of(suffix_ref)
    keys = jnp.concatenate([k_pre, k_suf], axis=0)
    values = jnp.concatenate([v_pre, v_suf], axis=0)
    tri = triangle()
    tiles = [(i, n) for i in range(q_ref.shape[0] // TILE) for n in range(GROUP_HEADS)]

    def place(tile):
        i, n = tile
        return slice(i * TILE, (i + 1) * TILE), slice(n * HEAD, (n + 1) * HEAD)

    def total(tile):
        return k_pre.shape[0] + (tile[0] + 1) * TILE

    def score(tile):
        q = q_ref[place(tile)]
        return lax.dot_general(q, keys[: total(tile)], (((1,), (1,)), ((), ())), preferred_element_type=jnp.float32)

    def weigh(tile, s):
        end = total(tile)
        s = jnp.concatenate([s[:, : end - TILE], jnp.where(tri, s[:, end - TILE :], NEG)], axis=1)
        top = jnp.max(s, axis=1, keepdims=True)
        return jnp.exp2((s - top) * SCALE).astype(jnp.bfloat16)

    def mix(tile, p):
        return jnp.dot(p, values[: total(tile)], preferred_element_type=jnp.float32)

    scores, weights, mixed = {}, {}, {}
    for t in range(len(tiles) + 3 * DEPTH):
        if t < len(tiles):
            scores[t] = score(tiles[t])
        u = t - DEPTH
        if 0 <= u < len(tiles):
            weights[u] = weigh(tiles[u], scores.pop(u))
        u -= DEPTH
        if 0 <= u < len(tiles):
            mixed[u] = mix(tiles[u], weights.pop(u))
        u -= DEPTH
        if 0 <= u < len(tiles):
            acc = mixed.pop(u)
            o_ref[place(tiles[u])] = (acc[:, :HEAD] / acc[:, HEAD:]).astype(jnp.bfloat16)


def cost(heads, keys):
    work = heads * GROUP_HEADS * 384 * keys
    return pl.CostEstimate(flops=4 * HEAD * work, bytes_accessed=heads * MIB * 3 // 2, transcendentals=work)


def attend(chunk, queries, pulled, suffix, page_count, so_far):
    first, heads = chunk
    tokens, width = queries.shape
    pages = pulled.shape[0]
    block = GROUP_HEADS * HEAD
    operands = [queries, pulled, suffix, page_count]
    in_specs = [
        pl.BlockSpec((tokens, block), lambda h: (0, first + h)),
        pl.BlockSpec((pages, 2, PAGE, HEAD), lambda h: (0, 0, 0, h)),
        pl.BlockSpec((2, tokens, HEAD), lambda h: (0, 0, first + h)),
        pl.BlockSpec(memory_space=SMEM),
    ]
    aliases = {}
    if so_far is not None:
        aliases = {len(operands): 0}
        operands.append(so_far)
        in_specs.append(pl.BlockSpec(memory_space=pl.ANY))
    return pl.pallas_call(
        attend_kernel,
        out_shape=jax.ShapeDtypeStruct((tokens, width), jnp.bfloat16),
        grid=(heads,),
        in_specs=in_specs,
        out_specs=pl.BlockSpec((tokens, block), lambda h: (0, first + h)),
        input_output_aliases=aliases,
        compiler_params=pltpu.CompilerParams(vmem_limit_bytes=63 * MIB + 480 * 1024),
        cost_estimate=cost(heads, 768),
        name="attend",
    )(*operands)


def shift(page, dy, dx):
    pairs = [(y * 2 + x, (y + dy) % RING * 2 + (x + dx) % 2) for y in range(RING) for x in range(2)]
    return lax.ppermute(page, "grp", pairs)


def exchange(pages):
    return lax.all_to_all(pages, "ep", split_axis=0, concat_axis=0, tiled=True)


def local(queries, suffix_kv, slot_page_cache, holder, page_slots, page_count):
    lane = lax.axis_index("ep")
    slots = lax.dynamic_index_in_dim(page_slots, lane, axis=2, keepdims=False)
    q, suffix = queries[0, 0], suffix_kv[0, 0]
    arrived = []
    for pages in pack(holder, slots, slot_page_cache[0, 0]):
        got = {0: pages[0]}
        for s in ORDER:
            got[s] = shift(pages[s], *SHIFTS[s])
        arrived.append([got[s] for s in range(len(SHIFTS))])
    pulled = []
    for c in range(len(CHUNKS)):
        forward = select(ORDERS[c], holder, arrived[c])
        if TIE and c + 1 < len(CHUNKS):
            tied = [arrived[c + 1][s] for s in ORDER[:TIE]]
            forward, tied = lax.optimization_barrier((forward, tied))
            for s, t in zip(ORDER[:TIE], tied):
                arrived[c + 1][s] = t
        pulled.append(exchange(forward))
    out = None
    for c, chunk in enumerate(CHUNKS):
        out = attend(chunk, q, pulled[c], suffix, page_count, out)
    return out[None, None]


def solution(mesh):
    return jax.shard_map(
        local,
        mesh=mesh,
        in_specs=(
            P("grp", "ep", None, None),
            P("grp", "ep", None, None, None),
            P("grp", "ep", None, None, None, None),
            P(),
            P(),
            P(),
        ),
        out_specs=P("grp", "ep", None, None),
        check_vma=False,
    )
```
